32 devices in a mesh: row: 4 (over z), col: 4 (over x, core), dp: 2 (over y).
Axes of the slice: x: 2, y: 2, z: 4, core: 2. Of those that a mesh axis runs over, the one named last changes fastest.
Arguments:
- hidden_states: bfloat16 [2048, 1536], P(('dp', 'row'), 'col'), may hold values from -18 to 18
- w_query: bfloat16 [1536, 1536], P('col', 'row'), may hold values from -0.102062073 to 0.102062073
- w_key_value: bfloat16 [1536, 512], P('col'), may hold values from -0.102062073 to 0.102062073
- adapter_down: bfloat16 [128, 1536, 16], P('dp', 'col'), may hold values from -0.15625 to 0.15625
- adapter_up: bfloat16 [128, 16, 1536], P('dp', None, 'row'), may hold values from -1.5 to 1.5
- req_lengths: int32 [2, 8], replicated, may hold values from 1 to 160, 960 in all within a row
- req_adapter: int32 [2, 8], replicated, may hold values from 0 to 127, as said below
Outputs:
- attention: bfloat16 [2048, 1536], P(('dp', 'col'), 'row')
- kv_cache: bfloat16 [2048, 512], P(('dp', 'col'))
The draws below stay inside these ranges and needn't reach their ends.
Inputs may be any that keep to these rules, and one draw needn't show every extreme that they name: `req_lengths`: the lengths of one block sum to 960, and each block has a request of exactly 160 tokens. `req_adapter`: adapters k * 64 to (k + 1) * 64 - 1 are those of index k of dp; the requests of one block use adapters of one index of dp at most 4 times, and some index of dp is used exactly that often by every block.
All inputs are finite; a program needn't handle non-finite values.
Results may differ from the reference program's by a relative error of at most 0.0072.
Values may be sent and summed in bfloat16 or wider, within the bound.
A program may use at most 128 MiB of HBM per device.

```python
import math
import jax
import jax.numpy as jnp
import numpy as np
from jax import lax

D = 1536
HEADS = 12
KV_HEADS = 2
HEAD_DIM = 128
RANK = 16
ADP_DEV = 64
GROUP_TOK = 1024
PREFIX = 64
REQ_DEV = 8
MOST_LEN = 160
ADAPTERS = 128
TOKENS = 2048
N_DP = 2


def draw_hidden_states(key, part):
    base_key = jax.random.fold_in(key, 7)
    drawn_rows = jnp.clip(jax.random.normal(jax.random.fold_in(base_key, 1), (TOKENS, D), jnp.float32), -6.0, 6.0)
    return drawn_rows.astype(jnp.bfloat16)


def weight_pair(key):
    base_key = jax.random.fold_in(key, 101)
    key_cols = jnp.clip(jax.random.normal(jax.random.fold_in(base_key, 1), (D, KV_HEADS * HEAD_DIM), jnp.float32), -4.0, 4.0) / math.sqrt(D)
    value_cols = jnp.clip(jax.random.normal(jax.random.fold_in(base_key, 2), (D, KV_HEADS * HEAD_DIM), jnp.float32), -4.0, 4.0) / math.sqrt(D)
    noise_cols = jnp.clip(jax.random.normal(jax.random.fold_in(base_key, 3), (D, HEADS * HEAD_DIM), jnp.float32), -4.0, 4.0) / math.sqrt(D)
    query_cols = noise_cols
    return (query_cols, jnp.concatenate([key_cols, value_cols], axis=1))


def draw_w_query(key, part):
    return weight_pair(key)[0].astype(jnp.bfloat16)


def draw_w_key_value(key, part):
    return weight_pair(key)[1].astype(jnp.bfloat16)


def draw_req_adapter(key, part):
    base_key = jax.random.fold_in(key, 13)
    offset_dp = jax.random.randint(jax.random.fold_in(base_key, 1), (), 0, N_DP)
    block_keys = jax.random.split(jax.random.fold_in(base_key, 2), N_DP)

    def block_ids(block_key):
        other_ids = jax.random.permutation(jax.random.fold_in(block_key, 1), N_DP - 1).astype(jnp.int32) + 1
        cycle_ids = jnp.concatenate([jnp.zeros((1,), jnp.int32), other_ids])
        req_order = jax.random.permutation(jax.random.fold_in(block_key, 2), REQ_DEV).astype(jnp.int32)
        holder_ids = (cycle_ids[req_order % N_DP] + offset_dp) % N_DP
        adapter_pick = jax.random.randint(jax.random.fold_in(block_key, 3), (REQ_DEV,), 0, ADP_DEV)
        return (holder_ids * ADP_DEV + adapter_pick).astype(jnp.int32)
    return jax.vmap(block_ids)(block_keys)


def shard_levels(own_key, dims, cuts, low, high):
    level = 1.0
    for position, shards_of in cuts:
        heights = jax.random.uniform(jax.random.fold_in(jax.random.fold_in(own_key, 6), position), (shards_of,), jnp.float32, low / len(cuts), high / len(cuts))
        level = level * jnp.repeat(jnp.exp(heights), dims[position] // shards_of).reshape((-1,) + (1,) * (len(dims) - 1 - position))
    return level


def length_profile(number_of, total, most, slope):
    loads = [(1 << 20) // math.isqrt(standing ** slope) + 1 for standing in range(2, number_of + 1)]
    surplus, holding = total - most - (number_of - 1), [1] * (number_of - 1)
    while surplus > 0:
        movable = [i for i in range(number_of - 1) if holding[i] < most]
        pool, budget = sum([loads[i] for i in movable]), surplus
        for i in movable:
            addition = min(most - holding[i], max(1, budget * loads[i] // pool), surplus)
            holding[i] = holding[i] + addition
            surplus = surplus - addition
    return np.array([most] + holding)


def uneven(stream_key, number_of, total, reach, slope):
    if number_of == 2:
        one = jax.random.randint(stream_key, (), max(1, total - reach), min(reach, total - 1) + 1)
        return jnp.stack([one, total - one])
    tallies = jnp.asarray(length_profile(number_of, total, reach, slope), jnp.int32)
    pairs = (number_of - 1) // 2
    giver, sink = tallies[1:1 + 2 * pairs:2], tallies[2:2 + 2 * pairs:2]
    slack = jnp.minimum(giver - 1, reach - sink)
    passed = jax.random.randint(jax.random.fold_in(stream_key, 1), (pairs,), 0, 1 << 20) % (slack + 1)
    tallies = tallies.at[1:1 + 2 * pairs:2].set(giver - passed).at[2:2 + 2 * pairs:2].set(sink + passed)
    return tallies[jax.random.permutation(jax.random.fold_in(stream_key, 2), number_of)]


def bell_draw(rng, dims, width, reach, shards=(), kind=jnp.bfloat16):
    result = width * jax.random.normal(rng, dims, jnp.float32)
    if shards:
        result = result * shard_levels(rng, dims, shards, -0.22, 0.18)
    return jnp.clip(result, -reach, reach).astype(kind)


def setup_inputs(seed: int = 0) -> dict:
    splits = jax.random.split(jax.random.key(seed), 8)
    return {
        "hidden_states": draw_hidden_states(jax.random.fold_in(splits[7], 71), 0),
        "w_query": draw_w_query(jax.random.fold_in(splits[7], 71), 0),
        "w_key_value": draw_w_key_value(jax.random.fold_in(splits[7], 71), 0),
        "adapter_down": bell_draw(splits[3], (ADAPTERS, D, RANK), D ** -0.5, 0.15625, ((0, 2), (1, 4))),
        "adapter_up": bell_draw(splits[4], (ADAPTERS, RANK, HEADS * HEAD_DIM), RANK ** -0.5, 1.5, ((0, 2), (2, 4))),
        "req_lengths": jax.vmap(lambda own: uneven(own, REQ_DEV, GROUP_TOK - PREFIX, MOST_LEN, 1))(jax.random.split(splits[5], N_DP)).reshape((N_DP, REQ_DEV)).astype(jnp.int32),
        "req_adapter": draw_req_adapter(jax.random.fold_in(splits[7], 71), 0),
    }


masked_score = -1e+30

def one_block(hidden, lengths_row, adapters_row, w_query, w_key_value, adapter_down, adapter_up):
    block_len = hidden.shape[0]
    requests = lengths_row.shape[0]
    prefix_len = (block_len - jnp.sum(lengths_row)).astype(jnp.int32)
    ends_at = (jnp.cumsum(lengths_row) + prefix_len).astype(jnp.int32)
    starts = (ends_at - lengths_row).astype(jnp.int32)
    positions = jnp.arange(block_len, dtype=jnp.int32)
    segment = lax.optimization_barrier(jnp.sum((positions[:, None] >= starts[None, :]).astype(jnp.int32), axis=1)).astype(jnp.int32)
    chosen_down = jnp.transpose(adapter_down[adapters_row], (1, 0, 2)).reshape(D, requests * RANK)
    chosen_up = adapter_up[adapters_row].reshape(requests * RANK, HEADS * HEAD_DIM).astype(jnp.float32)
    reduced = jnp.dot(hidden, chosen_down, preferred_element_type=jnp.float32)
    kept_cols = (jnp.arange(requests * RANK, dtype=jnp.int32) // RANK)[None, :] == (segment - 1)[:, None]
    reduced = jnp.where(kept_cols, reduced, jnp.float32(0.0))
    adapter_term = jnp.dot(reduced, chosen_up, precision=lax.Precision.HIGHEST)
    query_rows = (jnp.dot(hidden, w_query, preferred_element_type=jnp.float32) + adapter_term).astype(jnp.bfloat16)
    kv_cache = jnp.dot(hidden, w_key_value, preferred_element_type=jnp.float32).astype(jnp.bfloat16)
    allowed = (positions[None, :] <= positions[:, None]) & ((segment[None, :] == segment[:, None]) | (segment[None, :] == 0))
    per_group = HEADS // KV_HEADS
    kv_width = KV_HEADS * HEAD_DIM
    score_scale = 1.0 / math.sqrt(HEAD_DIM)

    def one_head(head_index):
        kv_group = head_index // per_group
        query_head = lax.dynamic_slice_in_dim(query_rows, head_index * HEAD_DIM, HEAD_DIM, 1)
        key_head = lax.dynamic_slice_in_dim(kv_cache, kv_group * HEAD_DIM, HEAD_DIM, 1)
        value_head = lax.dynamic_slice_in_dim(kv_cache, kv_width + kv_group * HEAD_DIM, HEAD_DIM, 1)
        scores = jnp.dot(query_head, key_head.T, preferred_element_type=jnp.float32) * score_scale
        scores = jnp.where(allowed, scores, masked_score)
        row_max = lax.optimization_barrier(jnp.max(scores, axis=1, keepdims=True))
        exponent = jnp.where(allowed, jnp.exp(scores - row_max), jnp.float32(0.0))
        row_sum = lax.optimization_barrier(jnp.sum(exponent, axis=1, keepdims=True))
        head_out = jnp.dot(exponent.astype(jnp.bfloat16), value_head, preferred_element_type=jnp.float32) / row_sum
        return head_out.astype(jnp.bfloat16)
    heads_out = lax.map(one_head, jnp.arange(HEADS, dtype=jnp.int32))
    attention = jnp.transpose(heads_out, (1, 0, 2)).reshape(block_len, HEADS * HEAD_DIM)
    return (attention, kv_cache)

def reference(hidden_states, w_query, w_key_value, adapter_down, adapter_up, req_lengths, req_adapter):
    blocks = hidden_states.reshape(N_DP, GROUP_TOK, D)

    def run_block(block_items):
        return one_block(block_items[0], block_items[1], block_items[2], w_query, w_key_value, adapter_down, adapter_up)
    attention, kv_cache = lax.map(run_block, (blocks, req_lengths, req_adapter))
    return (attention.reshape(TOKENS, HEADS * HEAD_DIM), kv_cache.reshape(TOKENS, 2 * KV_HEADS * HEAD_DIM))
```

```python
import functools
import math

import jax
import jax.numpy as jnp
from jax import lax
from jax.experimental import pallas as pl
from jax.experimental.pallas import tpu as pltpu
from jax.sharding import PartitionSpec as P

HEAD_DIM = 128
HEADS = 12
KV_HEADS = 2
PREFIX = 64
MESH = pl.DeviceIdType.MESH
FAR = 1 << 20


def remote(src, dst, send_sem, recv_sem, device):
    return pltpu.make_async_remote_copy(
        src_ref=src,
        dst_ref=dst,
        send_sem=send_sem,
        recv_sem=recv_sem,
        device_id=device,
        device_id_type=MESH,
    )


def kernel(
    n_dp,
    h_ref,
    wq_ref,
    wkv_ref,
    dn_ref,
    up_ref,
    len_ref,
    ad_ref,
    att_ref,
    kv_ref,
    hbuf,
    aout,
    ain,
    dsel,
    usel,
    rs_out,
    rs_in,
    keys,
    other,
    a_send,
    a_recv,
    h_send,
    h_recv,
    rs_send,
    rs_recv,
    k_send,
    k_recv,
):
    f32, bf16 = jnp.float32, jnp.bfloat16
    r = lax.axis_index("row")
    c = lax.axis_index("col")
    me = lax.axis_index("dp")
    rows = h_ref.shape[0]
    held, rank = dn_ref.shape[0], dn_ref.shape[1]
    per = ain.shape[1]
    requests = len_ref.shape[1]
    qcols = wq_ref.shape[1]
    block_len = 4 * rows
    back = rows - PREFIX
    sibling = c + 1 - 2 * lax.rem(c, 2)
    across = lax.rem(c + 2, 4)

    barrier = pltpu.get_barrier_semaphore()
    for j in range(1, 4):
        pl.semaphore_signal(
            barrier, inc=1, device_id={"row": lax.rem(r + j, 4)}, device_id_type=MESH
        )
        pl.semaphore_signal(
            barrier, inc=1, device_id={"col": lax.rem(c + j, 4)}, device_id_type=MESH
        )
    for j in range(1, n_dp):
        pl.semaphore_signal(
            barrier, inc=1, device_id={"dp": lax.rem(me + j, n_dp)}, device_id_type=MESH
        )

    def pick(target, store):
        first = me * held
        count = jnp.int32(0)
        picked = [jnp.int32(0)] * per
        for i in range(requests):
            adapter = ad_ref[target, i]
            mine = (adapter >= first) & (adapter < first + held)
            for k in range(per):
                picked[k] = jnp.where(mine & (count == k), adapter - first, picked[k])
            count = count + mine.astype(jnp.int32)
        for k in range(per):
            store(k, dn_ref[picked[k]], up_ref[picked[k]])

    def keep_own(k, down, up):
        ain[me, k, 0] = down
        ain[me, k, 1] = up

    pick(me, keep_own)
    for j in range(1, n_dp):

        def keep_out(k, down, up, j=j):
            aout[j - 1, k, 0] = down
            aout[j - 1, k, 1] = up

        pick(lax.rem(me + j, n_dp), keep_out)
    hbuf[r] = h_ref[...]

    pl.semaphore_wait(barrier, 6 + n_dp - 1)
    copies = []
    for j in range(1, n_dp):
        copies.append(
            remote(
                aout.at[j - 1],
                ain.at[me],
                a_send.at[j - 1],
                a_recv.at[j - 1],
                {"dp": lax.rem(me + j, n_dp)},
            )
        )
    for j in (2, 1, 3):
        copies.append(
            remote(
                h_ref,
                hbuf.at[r],
                h_send.at[j - 1],
                h_recv.at[j - 1],
                {"row": lax.rem(r + j, 4)},
            )
        )
    for copy in copies:
        copy.start()

    total = jnp.int32(0)
    for i in range(requests):
        total = total + len_ref[me, i]
    prefix = block_len - total
    starts, ends = [], []
    run = prefix
    for i in range(requests):
        starts.append(run)
        run = run + len_ref[me, i]
        ends.append(run)
    column = lax.broadcasted_iota(jnp.int32, (1, requests * rank), 1)
    col_start = jnp.zeros((1, requests * rank), jnp.int32)
    col_end = jnp.zeros((1, requests * rank), jnp.int32)
    for i in range(requests):
        here = (column >= i * rank) & (column < (i + 1) * rank)
        col_start = jnp.where(here, starts[i], col_start)
        col_end = jnp.where(here, ends[i], col_end)

    for copy in copies[: n_dp - 1]:
        copy.wait_recv()
    holders = [lax.div(ad_ref[me, i], held) for i in range(requests)]
    for i in range(requests):
        slot = jnp.int32(0)
        for j in range(i):
            slot = slot + (holders[j] == holders[i]).astype(jnp.int32)
        pair = ain[holders[i], jnp.minimum(slot, per - 1)]
        dsel[i * rank : (i + 1) * rank, :] = pair[0]
        usel[i * rank : (i + 1) * rank, :] = pair[1]

    group = lax.div(r * (HEADS // 4), HEADS // KV_HEADS)
    k_col = pl.multiple_of(group * HEAD_DIM, HEAD_DIM)
    v_col = pl.multiple_of((KV_HEADS + group) * HEAD_DIM, HEAD_DIM)
    k_oth = pl.multiple_of((1 - group) * HEAD_DIM, HEAD_DIM)
    v_oth = pl.multiple_of((KV_HEADS + 1 - group) * HEAD_DIM, HEAD_DIM)

    def part(b):
        step = lax.rem(r - b + 4, 4)

        @pl.when(step != 0)
        def _():
            at = lax.rem(step + 3, 4)
            remote(
                h_ref,
                hbuf.at[b],
                h_send.at[at],
                h_recv.at[at],
                {"row": lax.rem(r + 1, 4)},
            ).wait_recv()

        h = hbuf[b]
        low = lax.dot_general(
            h, dsel[...], (((1,), (1,)), ((), ())), preferred_element_type=f32
        )
        pos = b * rows + lax.broadcasted_iota(jnp.int32, (rows, 1), 0)
        low = jnp.where((pos >= col_start) & (pos < col_end), low, 0.0)
        high = low.astype(bf16)
        rest = (low - high.astype(f32)).astype(bf16)
        q = jnp.dot(h, wq_ref[...], preferred_element_type=f32)
        q = q + jnp.dot(high, usel[...], preferred_element_type=f32)
        q = q + jnp.dot(rest, usel[...], preferred_element_type=f32)
        k = jnp.dot(h, wkv_ref[:, pl.ds(k_col, HEAD_DIM)], preferred_element_type=f32)
        v = jnp.dot(h, wkv_ref[:, pl.ds(v_col, HEAD_DIM)], preferred_element_type=f32)
        return q, k, v

    def put(slot, terms):
        q, k, v = terms
        rs_out[slot, :, :qcols] = q.astype(bf16)
        rs_out[slot, :, qcols : qcols + HEAD_DIM] = k.astype(bf16)
        rs_out[slot, :, qcols + HEAD_DIM :] = v.astype(bf16)

    def plus(terms, slot):
        q, k, v = terms
        return (
            q + rs_in[slot, :, :qcols].astype(f32),
            k + rs_in[slot, :, qcols : qcols + HEAD_DIM].astype(f32),
            v + rs_in[slot, :, qcols + HEAD_DIM :].astype(f32),
        )

    def rs_copy(slot, device):
        return remote(
            rs_out.at[slot],
            rs_in.at[slot],
            rs_send.at[slot],
            rs_recv.at[slot],
            {"col": device},
        )

    to_relay = rs_copy(0, sibling)
    to_sibling = rs_copy(1, sibling)
    to_across = rs_copy(2, across)
    put(0, part(3 - c))
    to_relay.start()
    relayed = part(across)
    to_relay.wait_recv()
    put(2, plus(relayed, 0))
    to_across.start()
    put(1, part(sibling))
    to_sibling.start()
    own = part(c)
    to_sibling.wait_recv()
    own = plus(own, 1)
    to_across.wait_recv()
    q, k, v = plus(own, 2)
    q, k, v = q.astype(bf16), k.astype(bf16), v.astype(bf16)

    keys[rows:, :HEAD_DIM] = k
    keys[rows:, HEAD_DIM:] = v
    firsts = [
        remote(
            keys.at[pl.ds(rows, PREFIX)],
            keys.at[pl.ds(0, PREFIX)],
            k_send.at[j - 1],
            k_recv.at[0],
            {"col": lax.rem(c + j, 4)},
        )
        for j in range(1, 4)
    ]
    onward = remote(
        keys.at[pl.ds(rows + PREFIX, back)],
        keys.at[pl.ds(PREFIX, back)],
        k_send.at[3],
        k_recv.at[1],
        {"col": lax.rem(c + 1, 4)},
    )
    swap = remote(
        keys.at[pl.ds(rows, rows)],
        other,
        k_send.at[4],
        k_recv.at[2],
        {"row": lax.rem(r + 2, 4)},
    )

    @pl.when(c < 3)
    def _():
        onward.start()

    @pl.when(c == 0)
    def _():
        for copy in firsts:
            copy.start()
        keys[:rows, :] = jnp.zeros((rows, 2 * HEAD_DIM), bf16)

    swap.start()
    kv_ref[:, pl.ds(k_col, HEAD_DIM)] = k
    kv_ref[:, pl.ds(v_col, HEAD_DIM)] = v

    base = c * rows
    q_pos = base + lax.broadcasted_iota(jnp.int32, (rows, 1), 0)
    seg_start = jnp.zeros((rows, 1), jnp.int32)
    for i in range(requests):
        seg_start = jnp.where(q_pos >= starts[i], starts[i], seg_start)
    at = lax.broadcasted_iota(jnp.int32, (1, 2 * rows), 1)
    k_pos = jnp.where(at < PREFIX, at, base - rows + at)
    k_pos = jnp.where((at < rows) & (c == 0), FAR, k_pos)
    allowed = (k_pos <= q_pos) & ((k_pos >= seg_start) | (k_pos < prefix))

    @pl.when(c > 0)
    def _():
        firsts[0].wait_recv()
        onward.wait_recv()

    key_rows = keys[:, :HEAD_DIM]
    value_rows = keys[:, HEAD_DIM:]
    scale = 1.0 / math.sqrt(HEAD_DIM)
    for n in range(qcols // HEAD_DIM):
        cols = slice(n * HEAD_DIM, (n + 1) * HEAD_DIM)
        score = (
            lax.dot_general(
                q[:, cols], key_rows, (((1,), (1,)), ((), ())), preferred_element_type=f32
            )
            * scale
        )
        score = jnp.where(allowed, score, -1e30)
        weight = jnp.exp(score - jnp.max(score, axis=1, keepdims=True))
        weight = jnp.where(allowed, weight, 0.0)
        row_total = jnp.sum(weight, axis=1, keepdims=True)
        mixed = jnp.dot(weight.astype(bf16), value_rows, preferred_element_type=f32)
        att_ref[:, cols] = (mixed / row_total).astype(bf16)

    swap.wait_recv()
    kv_ref[:, pl.ds(k_oth, HEAD_DIM)] = other[:, :HEAD_DIM]
    kv_ref[:, pl.ds(v_oth, HEAD_DIM)] = other[:, HEAD_DIM:]

    for copy in copies:
        copy.wait_send()
    for copy in (to_relay, to_sibling, to_across, swap):
        copy.wait_send()

    @pl.when(c < 3)
    def _():
        onward.wait_send()

    @pl.when(c == 0)
    def _():
        for copy in firsts:
            copy.wait_send()


def body(hidden, w_query, w_key_value, adapter_down, adapter_up, req_lengths, req_adapter):
    n_dp = lax.axis_size("dp")
    rows, width = hidden.shape
    qcols = w_query.shape[1]
    rank = adapter_down.shape[2]
    requests = req_lengths.shape[1]
    per = (requests + n_dp - 1) // n_dp
    sums = qcols + 2 * HEAD_DIM
    bf16 = jnp.bfloat16
    vmem = pl.BlockSpec(memory_space=pltpu.VMEM)
    smem = pl.BlockSpec(memory_space=pltpu.SMEM)
    dma = pltpu.SemaphoreType.DMA
    return pl.pallas_call(
        functools.partial(kernel, n_dp),
        out_shape=(
            jax.ShapeDtypeStruct((rows, qcols), bf16),
            jax.ShapeDtypeStruct((rows, w_key_value.shape[1]), bf16),
        ),
        in_specs=[vmem] * 5 + [smem] * 2,
        out_specs=(vmem, vmem),
        scratch_shapes=[
            pltpu.VMEM((4, rows, width), bf16),
            pltpu.VMEM((n_dp - 1, per, 2, rank, width), bf16),
            pltpu.VMEM((n_dp, per, 2, rank, width), bf16),
            pltpu.VMEM((requests * rank, width), bf16),
            pltpu.VMEM((requests * rank, qcols), bf16),
            pltpu.VMEM((3, rows, sums), bf16),
            pltpu.VMEM((3, rows, sums), bf16),
            pltpu.VMEM((2 * rows, 2 * HEAD_DIM), bf16),
            pltpu.VMEM((rows, 2 * HEAD_DIM), bf16),
            dma((n_dp - 1,)),
            dma((n_dp - 1,)),
            dma((3,)),
            dma((3,)),
            dma((3,)),
            dma((3,)),
            dma((5,)),
            dma((3,)),
        ],
        compiler_params=pltpu.CompilerParams(
            collective_id=0, has_side_effects=True, vmem_limit_bytes=48 << 20
        ),
    )(
        hidden,
        w_query,
        w_key_value,
        jnp.transpose(adapter_down, (0, 2, 1)),
        adapter_up,
        req_lengths,
        req_adapter,
    )


def solution(mesh):
    return jax.shard_map(
        body,
        mesh=mesh,
        in_specs=(
            P(("dp", "row"), "col"),
            P("col", "row"),
            P("col", None),
            P("dp", "col", None),
            P("dp", None, "row"),
            P(),
            P(),
        ),
        out_specs=(P(("dp", "col"), "row"), P(("dp", "col"), None)),
        check_vma=False,
    )
```

```python
import functools
import math

import jax
import jax.numpy as jnp
from jax import lax
from jax.experimental import pallas as pl
from jax.experimental.pallas import tpu as pltpu
from jax.sharding import PartitionSpec as P

HEAD_DIM = 128
HEADS = 12
KV_HEADS = 2
PREFIX = 64
MESH = pl.DeviceIdType.MESH
FAR = 1 << 20


def remote(src, dst, send_sem, recv_sem, device):
    return pltpu.make_async_remote_copy(
        src_ref=src,
        dst_ref=dst,
        send_sem=send_sem,
        recv_sem=recv_sem,
        device_id=device,
        device_id_type=MESH,
    )


def kernel(
    n_dp,
    h_hbm,
    wq_hbm,
    wkv_hbm,
    dn_hbm,
    up_hbm,
    len_hbm,
    ad_hbm,
    att_ref,
    kv_ref,
    wq_ref,
    wkv_ref,
    dn_ref,
    up_ref,
    len_ref,
    ad_ref,
    loads,
    hbuf,
    aout,
    ain,
    dsel,
    usel,
    rs_out,
    rs_in,
    keys,
    other,
    mine_sum,
    a_send,
    a_recv,
    h_send,
    h_recv,
    rs_send,
    rs_recv,
    k_send,
    k_recv,
):
    f32, bf16 = jnp.float32, jnp.bfloat16
    r = lax.axis_index("row")
    c = lax.axis_index("col")
    me = lax.axis_index("dp")
    rows = h_hbm.shape[0]
    held, rank = dn_ref.shape[0], dn_ref.shape[1]
    per = ain.shape[1]
    requests = len_ref.shape[1]
    qcols = wq_ref.shape[1]
    block_len = 4 * rows
    back = rows - PREFIX
    sibling = c + 1 - 2 * lax.rem(c, 2)
    across = lax.rem(c + 2, 4)
    group = lax.div(r * (HEADS // 4), HEADS // KV_HEADS)
    k_col = pl.multiple_of(group * HEAD_DIM, HEAD_DIM)
    v_col = pl.multiple_of((KV_HEADS + group) * HEAD_DIM, HEAD_DIM)
    k_oth = pl.multiple_of((1 - group) * HEAD_DIM, HEAD_DIM)
    v_oth = pl.multiple_of((KV_HEADS + 1 - group) * HEAD_DIM, HEAD_DIM)

    def load(n, src, dst):
        copy = pltpu.make_async_copy(src, dst, loads.at[n])
        copy.start()
        return copy

    get_ad = load(0, ad_hbm, ad_ref)
    get_h = load(1, h_hbm, hbuf.at[r])
    get_dn = load(2, dn_hbm, dn_ref)
    get_up = load(3, up_hbm, up_ref)
    get_len = load(4, len_hbm, len_ref)
    get_wq = load(5, wq_hbm, wq_ref)
    get_k = load(6, wkv_hbm.at[:, pl.ds(k_col, HEAD_DIM)], wkv_ref.at[:, pl.ds(0, HEAD_DIM)])
    get_v = load(
        7, wkv_hbm.at[:, pl.ds(v_col, HEAD_DIM)], wkv_ref.at[:, pl.ds(HEAD_DIM, HEAD_DIM)]
    )

    barrier = pltpu.get_barrier_semaphore()
    for j in range(1, 4):
        pl.semaphore_signal(
            barrier, inc=1, device_id={"row": lax.rem(r + j, 4)}, device_id_type=MESH
        )
        pl.semaphore_signal(
            barrier, inc=1, device_id={"col": lax.rem(c + j, 4)}, device_id_type=MESH
        )
    for j in range(1, n_dp):
        pl.semaphore_signal(
            barrier, inc=1, device_id={"dp": lax.rem(me + j, n_dp)}, device_id_type=MESH
        )

    def pick(target, store):
        first = me * held
        count = jnp.int32(0)
        picked = [jnp.int32(0)] * per
        for i in range(requests):
            adapter = ad_ref[target, i]
            mine = (adapter >= first) & (adapter < first + held)
            for k in range(per):
                picked[k] = jnp.where(mine & (count == k), adapter - first, picked[k])
            count = count + mine.astype(jnp.int32)
        for k in range(per):
            store(k, dn_ref[picked[k]], up_ref[picked[k]])

    def keep_own(k, down, up):
        ain[me, k, 0] = down
        ain[me, k, 1] = up

    get_ad.wait()
    get_dn.wait()
    get_up.wait()
    for j in range(1, n_dp):

        def keep_out(k, down, up, j=j):
            aout[j - 1, k, 0] = down
            aout[j - 1, k, 1] = up

        pick(lax.rem(me + j, n_dp), keep_out)
    get_h.wait()

    def pass_on(b, sem, up_row):
        return remote(
            hbuf.at[b], hbuf.at[b], h_send.at[sem], h_recv.at[b], {"row": lax.rem(r + up_row, 4)}
        )

    pl.semaphore_wait(barrier, 6 + n_dp - 1)

    @pl.when(r < 3)
    def _():
        pass_on(r, 4, 1).start()

    @pl.when(r > 0)
    def _():
        pass_on(r, 5, 3).start()

    copies = []
    for j in range(1, n_dp):
        copies.append(
            remote(
                aout.at[j - 1],
                ain.at[me],
                a_send.at[j - 1],
                a_recv.at[j - 1],
                {"dp": lax.rem(me + j, n_dp)},
            )
        )
    for copy in copies:
        copy.start()
    pick(me, keep_own)
    get_len.wait()

    total = jnp.int32(0)
    for i in range(requests):
        total = total + len_ref[me, i]
    prefix = block_len - total
    starts, ends = [], []
    run = prefix
    for i in range(requests):
        starts.append(run)
        run = run + len_ref[me, i]
        ends.append(run)
    column = lax.broadcasted_iota(jnp.int32, (1, requests * rank), 1)
    col_start = jnp.zeros((1, requests * rank), jnp.int32)
    col_end = jnp.zeros((1, requests * rank), jnp.int32)
    for i in range(requests):
        here = (column >= i * rank) & (column < (i + 1) * rank)
        col_start = jnp.where(here, starts[i], col_start)
        col_end = jnp.where(here, ends[i], col_end)

    for copy in copies:
        copy.wait_recv()
    holders = [lax.div(ad_ref[me, i], held) for i in range(requests)]
    for i in range(requests):
        slot = jnp.int32(0)
        for j in range(i):
            slot = slot + (holders[j] == holders[i]).astype(jnp.int32)
        pair = ain[holders[i], jnp.minimum(slot, per - 1)]
        dsel[i * rank : (i + 1) * rank, :] = pair[0]
        usel[i * rank : (i + 1) * rank, :] = pair[1]

    get_wq.wait()
    get_k.wait()
    get_v.wait()

    def part(b):
        @pl.when(b != r)
        def _():
            pass_on(b, b, 1).wait_recv()

        @pl.when((b < r) & (r < 3))
        def _():
            pass_on(b, b, 1).start()

        @pl.when((b > r) & (r > 0))
        def _():
            pass_on(b, b, 3).start()

        h = hbuf[b]
        low = lax.dot_general(
            h, dsel[...], (((1,), (1,)), ((), ())), preferred_element_type=f32
        )
        pos = b * rows + lax.broadcasted_iota(jnp.int32, (rows, 1), 0)
        low = jnp.where((pos >= col_start) & (pos < col_end), low, 0.0)
        high = low.astype(bf16)
        rest = (low - high.astype(f32)).astype(bf16)
        q = jnp.dot(h, wq_ref[...], preferred_element_type=f32)
        q = q + jnp.dot(high, usel[...], preferred_element_type=f32)
        q = q + jnp.dot(rest, usel[...], preferred_element_type=f32)
        return q, jnp.dot(h, wkv_ref[...], preferred_element_type=f32)

    def put(slot, terms):
        rs_out[slot, :, :qcols] = terms[0].astype(bf16)
        rs_out[slot, :, qcols:] = terms[1].astype(bf16)

    def plus(terms, slot):
        return (
            terms[0] + rs_in[slot, :, :qcols].astype(f32),
            terms[1] + rs_in[slot, :, qcols:].astype(f32),
        )

    def rs_copy(slot, device):
        return remote(
            rs_out.at[slot],
            rs_in.at[slot],
            rs_send.at[slot],
            rs_recv.at[slot],
            {"col": device},
        )

    half = lax.div(r, 2)
    inner = r + half * (3 - 2 * r)
    for step in range(4):
        b = step + inner * (1 - 2 * step) if step < 2 else step + 0 * r
        b = b + half * (3 - 2 * b)
        odd = lax.rem(c + b, 2)
        far = lax.rem(lax.div(c, 2) + lax.div(b, 2), 2)
        terms = part(b)

        @pl.when(odd == 1)
        def _():
            put(1 - far, terms)
            rs_copy(1 - far, sibling).start()

        @pl.when((odd == 0) & (far == 1))
        def _():
            rs_copy(0, sibling).wait_recv()
            put(2, plus(terms, 0))
            rs_copy(2, across).start()

        @pl.when(c == b)
        def _():
            mine_sum[:, :qcols] = terms[0]
            mine_sum[:, qcols:] = terms[1]

    rs_copy(1, sibling).wait_recv()
    own = plus((mine_sum[:, :qcols], mine_sum[:, qcols:]), 1)
    rs_copy(2, across).wait_recv()
    q, kv = plus(own, 2)
    q, kv = q.astype(bf16), kv.astype(bf16)

    keys[rows:, :] = kv
    firsts = [
        remote(
            keys.at[pl.ds(rows, PREFIX)],
            keys.at[pl.ds(0, PREFIX)],
            k_send.at[j - 1],
            k_recv.at[0],
            {"col": lax.rem(c + j, 4)},
        )
        for j in range(1, 4)
    ]
    onward = remote(
        keys.at[pl.ds(rows + PREFIX, back)],
        keys.at[pl.ds(PREFIX, back)],
        k_send.at[3],
        k_recv.at[1],
        {"col": lax.rem(c + 1, 4)},
    )
    swap = remote(
        keys.at[pl.ds(rows, rows)],
        other,
        k_send.at[4],
        k_recv.at[2],
        {"row": lax.rem(r + 2, 4)},
    )

    @pl.when(c < 3)
    def _():
        onward.start()

    @pl.when(c == 0)
    def _():
        for copy in firsts:
            copy.start()
        keys[:rows, :] = jnp.zeros((rows, 2 * HEAD_DIM), bf16)

    swap.start()
    kv_ref[:, pl.ds(k_col, HEAD_DIM)] = kv[:, :HEAD_DIM]
    kv_ref[:, pl.ds(v_col, HEAD_DIM)] = kv[:, HEAD_DIM:]

    base = c * rows
    q_pos = base + lax.broadcasted_iota(jnp.int32, (rows, 1), 0)
    seg_start = jnp.zeros((rows, 1), jnp.int32)
    for i in range(requests):
        seg_start = jnp.where(q_pos >= starts[i], starts[i], seg_start)
    at = lax.broadcasted_iota(jnp.int32, (1, 2 * rows), 1)
    k_pos = jnp.where(at < PREFIX, at, base - rows + at)
    k_pos = jnp.where((at < rows) & (c == 0), FAR, k_pos)
    allowed = (k_pos <= q_pos) & ((k_pos >= seg_start) | (k_pos < prefix))

    @pl.when(c > 0)
    def _():
        firsts[0].wait_recv()
        onward.wait_recv()

    key_rows = keys[:, :HEAD_DIM]
    value_rows = keys[:, HEAD_DIM:]
    scale = 1.0 / math.sqrt(HEAD_DIM)
    for n in range(qcols // HEAD_DIM):
        cols = slice(n * HEAD_DIM, (n + 1) * HEAD_DIM)
        score = (
            lax.dot_general(
                q[:, cols], key_rows, (((1,), (1,)), ((), ())), preferred_element_type=f32
            )
            * scale
        )
        score = jnp.where(allowed, score, -1e30)
        weight = jnp.exp(score - jnp.max(score, axis=1, keepdims=True))
        weight = jnp.where(allowed, weight, 0.0)
        row_total = jnp.sum(weight, axis=1, keepdims=True)
        mixed = jnp.dot(weight.astype(bf16), value_rows, preferred_element_type=f32)
        att_ref[:, cols] = (mixed / row_total).astype(bf16)

    swap.wait_recv()
    kv_ref[:, pl.ds(k_oth, HEAD_DIM)] = other[:, :HEAD_DIM]
    kv_ref[:, pl.ds(v_oth, HEAD_DIM)] = other[:, HEAD_DIM:]

    for copy in copies:
        copy.wait_send()
    for copy in (rs_copy(0, sibling), rs_copy(1, sibling), rs_copy(2, across), swap):
        copy.wait_send()

    @pl.when(r < 3)
    def _():
        pass_on(r, 4, 1).wait_send()

    @pl.when(r > 0)
    def _():
        pass_on(r, 5, 3).wait_send()

    for b in range(4):

        @pl.when(((b < r) & (r < 3)) | ((b > r) & (r > 0)))
        def _():
            pass_on(b, b, 1).wait_send()

    @pl.when(c < 3)
    def _():
        onward.wait_send()

    @pl.when(c == 0)
    def _():
        for copy in firsts:
            copy.wait_send()


def body(hidden, w_query, w_key_value, adapter_down, adapter_up, req_lengths, req_adapter):
    n_dp = lax.axis_size("dp")
    rows, width = hidden.shape
    qcols = w_query.shape[1]
    rank = adapter_down.shape[2]
    requests = req_lengths.shape[1]
    per = (requests + n_dp - 1) // n_dp
    sums = qcols + 2 * HEAD_DIM
    bf16 = jnp.bfloat16
    vmem = pl.BlockSpec(memory_space=pltpu.VMEM)
    dma = pltpu.SemaphoreType.DMA
    return pl.pallas_call(
        functools.partial(kernel, n_dp),
        out_shape=(
            jax.ShapeDtypeStruct((rows, qcols), bf16),
            jax.ShapeDtypeStruct((rows, w_key_value.shape[1]), bf16),
        ),
        in_specs=[pl.BlockSpec(memory_space=pltpu.HBM)] * 7,
        out_specs=(vmem, vmem),
        scratch_shapes=[
            pltpu.VMEM(w_query.shape, bf16),
            pltpu.VMEM((width, 2 * HEAD_DIM), bf16),
            pltpu.VMEM((adapter_down.shape[0], rank, width), bf16),
            pltpu.VMEM(adapter_up.shape, bf16),
            pltpu.SMEM(req_lengths.shape, jnp.int32),
            pltpu.SMEM(req_adapter.shape, jnp.int32),
            dma((8,)),
            pltpu.VMEM((4, rows, width), bf16),
            pltpu.VMEM((n_dp - 1, per, 2, rank, width), bf16),
            pltpu.VMEM((n_dp, per, 2, rank, width), bf16),
            pltpu.VMEM((requests * rank, width), bf16),
            pltpu.VMEM((requests * rank, qcols), bf16),
            pltpu.VMEM((3, rows, sums), bf16),
            pltpu.VMEM((3, rows, sums), bf16),
            pltpu.VMEM((2 * rows, 2 * HEAD_DIM), bf16),
            pltpu.VMEM((rows, 2 * HEAD_DIM), bf16),
            pltpu.VMEM((rows, sums), jnp.float32),
            dma((n_dp - 1,)),
            dma((n_dp - 1,)),
            dma((6,)),
            dma((4,)),
            dma((3,)),
            dma((3,)),
            dma((5,)),
            dma((3,)),
        ],
        compiler_params=pltpu.CompilerParams(
            collective_id=0, has_side_effects=True, vmem_limit_bytes=60 << 20
        ),
    )(
        hidden,
        w_query,
        w_key_value,
        jnp.transpose(adapter_down, (0, 2, 1)),
        adapter_up,
        req_lengths,
        req_adapter,
    )


def solution(mesh):
    return jax.shard_map(
        body,
        mesh=mesh,
        in_specs=(
            P(("dp", "row"), "col"),
            P("col", "row"),
            P("col", None),
            P("dp", "col", None),
            P("dp", None, "row"),
            P(),
            P(),
        ),
        out_specs=(P(("dp", "col"), "row"), P(("dp", "col"), None)),
        check_vma=False,
    )
```

```python
import functools
import math

import jax
import jax.numpy as jnp
from jax import lax
from jax.experimental import pallas as pl
from jax.experimental.pallas import tpu as pltpu
from jax.sharding import PartitionSpec as P

HEAD_DIM = 128
HEADS = 12
KV_HEADS = 2
PREFIX = 64
MESH = pl.DeviceIdType.MESH
FAR = 1 << 20


def remote(src, dst, send_sem, recv_sem, device):
    return pltpu.make_async_remote_copy(
        src_ref=src,
        dst_ref=dst,
        send_sem=send_sem,
        recv_sem=recv_sem,
        device_id=device,
        device_id_type=MESH,
    )


def kernel(
    n_dp,
    h_hbm,
    wq_hbm,
    wkv_hbm,
    dn_hbm,
    up_hbm,
    len_hbm,
    ad_hbm,
    att_ref,
    kv_ref,
    wq_ref,
    wkv_ref,
    dn_ref,
    up_ref,
    len_ref,
    ad_ref,
    loads,
    hbuf,
    aout,
    ain,
    dsel,
    usel,
    rs_out,
    rs_in,
    keys,
    other,
    mine_sum,
    a_send,
    a_recv,
    h_send,
    h_recv,
    rs_send,
    rs_recv,
    k_send,
    k_recv,
):
    f32, bf16 = jnp.float32, jnp.bfloat16
    r = lax.axis_index("row")
    c = lax.axis_index("col")
    me = lax.axis_index("dp")
    rows = h_hbm.shape[0]
    held, rank = dn_ref.shape[0], dn_ref.shape[1]
    per = ain.shape[1]
    requests = len_ref.shape[1]
    qcols = wq_ref.shape[1]
    block_len = 4 * rows
    back = rows - PREFIX
    sibling = c + 1 - 2 * lax.rem(c, 2)
    across = lax.rem(c + 2, 4)
    group = lax.div(r * (HEADS // 4), HEADS // KV_HEADS)
    k_col = pl.multiple_of(group * HEAD_DIM, HEAD_DIM)
    v_col = pl.multiple_of((KV_HEADS + group) * HEAD_DIM, HEAD_DIM)
    k_oth = pl.multiple_of((1 - group) * HEAD_DIM, HEAD_DIM)
    v_oth = pl.multiple_of((KV_HEADS + 1 - group) * HEAD_DIM, HEAD_DIM)

    def load(n, src, dst):
        copy = pltpu.make_async_copy(src, dst, loads.at[n])
        copy.start()
        return copy

    get_ad = load(0, ad_hbm, ad_ref)
    get_h = load(1, h_hbm, hbuf.at[r])
    get_dn = load(2, dn_hbm, dn_ref)
    get_up = load(3, up_hbm, up_ref)
    get_len = load(4, len_hbm, len_ref)
    get_wq = load(5, wq_hbm, wq_ref)
    get_k = load(6, wkv_hbm.at[:, pl.ds(k_col, HEAD_DIM)], wkv_ref.at[:, pl.ds(0, HEAD_DIM)])
    get_v = load(
        7, wkv_hbm.at[:, pl.ds(v_col, HEAD_DIM)], wkv_ref.at[:, pl.ds(HEAD_DIM, HEAD_DIM)]
    )

    barrier = pltpu.get_barrier_semaphore()
    for j in range(1, 4):
        pl.semaphore_signal(
            barrier, inc=1, device_id={"row": lax.rem(r + j, 4)}, device_id_type=MESH
        )
        pl.semaphore_signal(
            barrier, inc=1, device_id={"col": lax.rem(c + j, 4)}, device_id_type=MESH
        )
    for j in range(1, n_dp):
        pl.semaphore_signal(
            barrier, inc=1, device_id={"dp": lax.rem(me + j, n_dp)}, device_id_type=MESH
        )

    def pick(target, store):
        first = me * held
        count = jnp.int32(0)
        picked = [jnp.int32(0)] * per
        for i in range(requests):
            adapter = ad_ref[target, i]
            mine = (adapter >= first) & (adapter < first + held)
            for k in range(per):
                picked[k] = jnp.where(mine & (count == k), adapter - first, picked[k])
            count = count + mine.astype(jnp.int32)
        for k in range(per):
            store(k, dn_ref[picked[k]], up_ref[picked[k]])

    def keep_own(k, down, up):
        ain[me, k, 0] = down
        ain[me, k, 1] = up

    get_ad.wait()
    get_dn.wait()
    get_up.wait()
    for j in range(1, n_dp):

        def keep_out(k, down, up, j=j):
            aout[j - 1, k, 0] = down
            aout[j - 1, k, 1] = up

        pick(lax.rem(me + j, n_dp), keep_out)
    get_h.wait()

    def pass_on(b, sem, up_row):
        return remote(
            hbuf.at[b], hbuf.at[b], h_send.at[sem], h_recv.at[b], {"row": lax.rem(r + up_row, 4)}
        )

    pl.semaphore_wait(barrier, 6 + n_dp - 1)

    @pl.when(r < 3)
    def _():
        pass_on(r, 4, 1).start()

    @pl.when(r > 0)
    def _():
        pass_on(r, 5, 3).start()

    copies = []
    for j in range(1, n_dp):
        copies.append(
            remote(
                aout.at[j - 1],
                ain.at[me],
                a_send.at[j - 1],
                a_recv.at[j - 1],
                {"dp": lax.rem(me + j, n_dp)},
            )
        )
    for copy in copies:
        copy.start()
    pick(me, keep_own)
    get_len.wait()

    total = jnp.int32(0)
    for i in range(requests):
        total = total + len_ref[me, i]
    prefix = block_len - total
    starts, ends = [], []
    run = prefix
    for i in range(requests):
        starts.append(run)
        run = run + len_ref[me, i]
        ends.append(run)
    column = lax.broadcasted_iota(jnp.int32, (1, requests * rank), 1)
    col_start = jnp.zeros((1, requests * rank), jnp.int32)
    col_end = jnp.zeros((1, requests * rank), jnp.int32)
    for i in range(requests):
        here = (column >= i * rank) & (column < (i + 1) * rank)
        col_start = jnp.where(here, starts[i], col_start)
        col_end = jnp.where(here, ends[i], col_end)

    def take(b):
        @pl.when(b != r)
        def _():
            pass_on(b, b, 1).wait_recv()

        @pl.when((b < r) & (r < 3))
        def _():
            pass_on(b, b, 1).start()

        @pl.when((b > r) & (r > 0))
        def _():
            pass_on(b, b, 3).start()

    half = lax.div(r, 2)
    inner = r + half * (3 - 2 * r)
    order = []
    for step in range(4):
        b = step + inner * (1 - 2 * step) if step < 2 else step + 0 * r
        order.append(b + half * (3 - 2 * b))

    @pl.when(inner == 1)
    def _():
        take(order[1])
        take(order[2])

    for copy in copies:
        copy.wait_recv()
    holders = [lax.div(ad_ref[me, i], held) for i in range(requests)]
    for i in range(requests):
        slot = jnp.int32(0)
        for j in range(i):
            slot = slot + (holders[j] == holders[i]).astype(jnp.int32)
        pair = ain[holders[i], jnp.minimum(slot, per - 1)]
        dsel[i * rank : (i + 1) * rank, :] = pair[0]
        usel[i * rank : (i + 1) * rank, :] = pair[1]

    get_wq.wait()
    get_k.wait()
    get_v.wait()

    def part(b):
        h = hbuf[b]
        low = lax.dot_general(
            h, dsel[...], (((1,), (1,)), ((), ())), preferred_element_type=f32
        )
        pos = b * rows + lax.broadcasted_iota(jnp.int32, (rows, 1), 0)
        low = jnp.where((pos >= col_start) & (pos < col_end), low, 0.0)
        high = low.astype(bf16)
        rest = (low - high.astype(f32)).astype(bf16)
        q = jnp.dot(h, wq_ref[...], preferred_element_type=f32)
        q = q + jnp.dot(high, usel[...], preferred_element_type=f32)
        q = q + jnp.dot(rest, usel[...], preferred_element_type=f32)
        return q, jnp.dot(h, wkv_ref[...], preferred_element_type=f32)

    def put(slot, terms):
        rs_out[slot, :, :qcols] = terms[0].astype(bf16)
        rs_out[slot, :, qcols:] = terms[1].astype(bf16)

    def plus(terms, slot):
        return (
            terms[0] + rs_in[slot, :, :qcols].astype(f32),
            terms[1] + rs_in[slot, :, qcols:].astype(f32),
        )

    def rs_copy(slot, device):
        return remote(
            rs_out.at[slot],
            rs_in.at[slot],
            rs_send.at[slot],
            rs_recv.at[slot],
            {"col": device},
        )

    for step, b in enumerate(order):
        if step in (1, 2):

            @pl.when(inner == 0)
            def _():
                take(b)

        elif step == 3:
            take(b)
        odd = lax.rem(c + b, 2)
        far = lax.rem(lax.div(c, 2) + lax.div(b, 2), 2)
        terms = part(b)

        @pl.when(odd == 1)
        def _():
            put(1 - far, terms)
            rs_copy(1 - far, sibling).start()

        @pl.when((odd == 0) & (far == 1))
        def _():
            rs_copy(0, sibling).wait_recv()
            put(2, plus(terms, 0))
            rs_copy(2, across).start()

        @pl.when(c == b)
        def _():
            mine_sum[:, :qcols] = terms[0]
            mine_sum[:, qcols:] = terms[1]

    rs_copy(1, sibling).wait_recv()
    own = plus((mine_sum[:, :qcols], mine_sum[:, qcols:]), 1)
    rs_copy(2, across).wait_recv()
    q, kv = plus(own, 2)
    q, kv = q.astype(bf16), kv.astype(bf16)

    keys[rows:, :] = kv
    firsts = [
        remote(
            keys.at[pl.ds(rows, PREFIX)],
            keys.at[pl.ds(0, PREFIX)],
            k_send.at[j - 1],
            k_recv.at[0],
            {"col": lax.rem(c + j, 4)},
        )
        for j in range(1, 4)
    ]
    onward = remote(
        keys.at[pl.ds(rows + PREFIX, back)],
        keys.at[pl.ds(PREFIX, back)],
        k_send.at[3],
        k_recv.at[1],
        {"col": lax.rem(c + 1, 4)},
    )
    swap = remote(
        keys.at[pl.ds(rows, rows)],
        other,
        k_send.at[4],
        k_recv.at[2],
        {"row": lax.rem(r + 2, 4)},
    )

    @pl.when(c < 3)
    def _():
        onward.start()

    @pl.when(c == 0)
    def _():
        for copy in firsts:
            copy.start()
        keys[:rows, :] = jnp.zeros((rows, 2 * HEAD_DIM), bf16)

    swap.start()
    kv_ref[:, pl.ds(k_col, HEAD_DIM)] = kv[:, :HEAD_DIM]
    kv_ref[:, pl.ds(v_col, HEAD_DIM)] = kv[:, HEAD_DIM:]

    base = c * rows
    q_pos = base + lax.broadcasted_iota(jnp.int32, (rows, 1), 0)
    seg_start = jnp.zeros((rows, 1), jnp.int32)
    for i in range(requests):
        seg_start = jnp.where(q_pos >= starts[i], starts[i], seg_start)
    at = lax.broadcasted_iota(jnp.int32, (1, 2 * rows), 1)
    k_pos = jnp.where(at < PREFIX, at, base - rows + at)
    k_pos = jnp.where((at < rows) & (c == 0), FAR, k_pos)
    allowed = (k_pos <= q_pos) & ((k_pos >= seg_start) | (k_pos < prefix))

    @pl.when(c > 0)
    def _():
        firsts[0].wait_recv()
        onward.wait_recv()

    key_rows = keys[:, :HEAD_DIM]
    value_rows = keys[:, HEAD_DIM:]
    scale = 1.0 / math.sqrt(HEAD_DIM)
    for n in range(qcols // HEAD_DIM):
        cols = slice(n * HEAD_DIM, (n + 1) * HEAD_DIM)
        score = (
            lax.dot_general(
                q[:, cols], key_rows, (((1,), (1,)), ((), ())), preferred_element_type=f32
            )
            * scale
        )
        score = jnp.where(allowed, score, -1e30)
        weight = jnp.exp(score - jnp.max(score, axis=1, keepdims=True))
        weight = jnp.where(allowed, weight, 0.0)
        row_total = jnp.sum(weight, axis=1, keepdims=True)
        mixed = jnp.dot(weight.astype(bf16), value_rows, preferred_element_type=f32)
        att_ref[:, cols] = (mixed / row_total).astype(bf16)

    swap.wait_recv()
    kv_ref[:, pl.ds(k_oth, HEAD_DIM)] = other[:, :HEAD_DIM]
    kv_ref[:, pl.ds(v_oth, HEAD_DIM)] = other[:, HEAD_DIM:]

    for copy in copies:
        copy.wait_send()
    for copy in (rs_copy(0, sibling), rs_copy(1, sibling), rs_copy(2, across), swap):
        copy.wait_send()

    @pl.when(r < 3)
    def _():
        pass_on(r, 4, 1).wait_send()

    @pl.when(r > 0)
    def _():
        pass_on(r, 5, 3).wait_send()

    for b in range(4):

        @pl.when(((b < r) & (r < 3)) | ((b > r) & (r > 0)))
        def _():
            pass_on(b, b, 1).wait_send()

    @pl.when(c < 3)
    def _():
        onward.wait_send()

    @pl.when(c == 0)
    def _():
        for copy in firsts:
            copy.wait_send()


def body(hidden, w_query, w_key_value, adapter_down, adapter_up, req_lengths, req_adapter):
    n_dp = lax.axis_size("dp")
    rows, width = hidden.shape
    qcols = w_query.shape[1]
    rank = adapter_down.shape[2]
    requests = req_lengths.shape[1]
    per = (requests + n_dp - 1) // n_dp
    sums = qcols + 2 * HEAD_DIM
    bf16 = jnp.bfloat16
    vmem = pl.BlockSpec(memory_space=pltpu.VMEM)
    dma = pltpu.SemaphoreType.DMA
    return pl.pallas_call(
        functools.partial(kernel, n_dp),
        out_shape=(
            jax.ShapeDtypeStruct((rows, qcols), bf16),
            jax.ShapeDtypeStruct((rows, w_key_value.shape[1]), bf16),
        ),
        in_specs=[pl.BlockSpec(memory_space=pltpu.HBM)] * 7,
        out_specs=(vmem, vmem),
        scratch_shapes=[
            pltpu.VMEM(w_query.shape, bf16),
            pltpu.VMEM((width, 2 * HEAD_DIM), bf16),
            pltpu.VMEM((adapter_down.shape[0], rank, width), bf16),
            pltpu.VMEM(adapter_up.shape, bf16),
            pltpu.SMEM(req_lengths.shape, jnp.int32),
            pltpu.SMEM(req_adapter.shape, jnp.int32),
            dma((8,)),
            pltpu.VMEM((4, rows, width), bf16),
            pltpu.VMEM((n_dp - 1, per, 2, rank, width), bf16),
            pltpu.VMEM((n_dp, per, 2, rank, width), bf16),
            pltpu.VMEM((requests * rank, width), bf16),
            pltpu.VMEM((requests * rank, qcols), bf16),
            pltpu.VMEM((3, rows, sums), bf16),
            pltpu.VMEM((3, rows, sums), bf16),
            pltpu.VMEM((2 * rows, 2 * HEAD_DIM), bf16),
            pltpu.VMEM((rows, 2 * HEAD_DIM), bf16),
            pltpu.VMEM((rows, sums), jnp.float32),
            dma((n_dp - 1,)),
            dma((n_dp - 1,)),
            dma((6,)),
            dma((4,)),
            dma((3,)),
            dma((3,)),
            dma((5,)),
            dma((3,)),
        ],
        compiler_params=pltpu.CompilerParams(
            collective_id=0, has_side_effects=True, vmem_limit_bytes=60 << 20
        ),
    )(
        hidden,
        w_query,
        w_key_value,
        jnp.transpose(adapter_down, (0, 2, 1)),
        adapter_up,
        req_lengths,
        req_adapter,
    )


def solution(mesh):
    return jax.shard_map(
        body,
        mesh=mesh,
        in_specs=(
            P(("dp", "row"), "col"),
            P("col", "row"),
            P("col", None),
            P("dp", "col", None),
            P("dp", None, "row"),
            P(),
            P(),
        ),
        out_specs=(P(("dp", "col"), "row"), P(("dp", "col"), None)),
        check_vma=False,
    )
```

```python
import functools
import math

import jax
import jax.numpy as jnp
from jax import lax
from jax.experimental import pallas as pl
from jax.experimental.pallas import tpu as pltpu
from jax.sharding import PartitionSpec as P

HEAD_DIM = 128
HEADS = 12
KV_HEADS = 2
PREFIX = 64
MESH = pl.DeviceIdType.MESH
FAR = 1 << 20
PARTS = 2


def remote(src, dst, send_sem, recv_sem, device):
    return pltpu.make_async_remote_copy(
        src_ref=src,
        dst_ref=dst,
        send_sem=send_sem,
        recv_sem=recv_sem,
        device_id=device,
        device_id_type=MESH,
    )


def kernel(
    n_dp,
    h_hbm,
    wq_hbm,
    wkv_hbm,
    dn_hbm,
    up_hbm,
    len_hbm,
    ad_hbm,
    att_ref,
    kv_ref,
    wq_ref,
    wkv_ref,
    dn_ref,
    up_ref,
    len_ref,
    ad_ref,
    loads,
    hbuf,
    aout,
    ain,
    dsel,
    usel,
    rs_out,
    rs_in,
    keys,
    other,
    mine_sum,
    a_send,
    a_recv,
    h_send,
    h_recv,
    rs_send,
    rs_recv,
    k_send,
    k_recv,
):
    f32, bf16 = jnp.float32, jnp.bfloat16
    r = lax.axis_index("row")
    c = lax.axis_index("col")
    me = lax.axis_index("dp")
    rows = h_hbm.shape[0]
    held, rank = dn_ref.shape[0], dn_ref.shape[1]
    per = ain.shape[1]
    requests = len_ref.shape[1]
    qcols = wq_ref.shape[1]
    block_len = 4 * rows
    back = rows - PREFIX
    sibling = c + 1 - 2 * lax.rem(c, 2)
    across = lax.rem(c + 2, 4)
    group = lax.div(r * (HEADS // 4), HEADS // KV_HEADS)
    k_col = pl.multiple_of(group * HEAD_DIM, HEAD_DIM)
    v_col = pl.multiple_of((KV_HEADS + group) * HEAD_DIM, HEAD_DIM)
    k_oth = pl.multiple_of((1 - group) * HEAD_DIM, HEAD_DIM)
    v_oth = pl.multiple_of((KV_HEADS + 1 - group) * HEAD_DIM, HEAD_DIM)

    def load(n, src, dst):
        copy = pltpu.make_async_copy(src, dst, loads.at[n])
        copy.start()
        return copy

    get_ad = load(0, ad_hbm, ad_ref)
    get_h = load(1, h_hbm, hbuf.at[r])
    get_dn = load(2, dn_hbm, dn_ref)
    get_up = load(3, up_hbm, up_ref)
    get_len = load(4, len_hbm, len_ref)
    get_wq = load(5, wq_hbm, wq_ref)
    get_k = load(6, wkv_hbm.at[:, pl.ds(k_col, HEAD_DIM)], wkv_ref.at[:, pl.ds(0, HEAD_DIM)])
    get_v = load(
        7, wkv_hbm.at[:, pl.ds(v_col, HEAD_DIM)], wkv_ref.at[:, pl.ds(HEAD_DIM, HEAD_DIM)]
    )

    barrier = pltpu.get_barrier_semaphore()
    for j in range(1, 4):
        pl.semaphore_signal(
            barrier, inc=1, device_id={"row": lax.rem(r + j, 4)}, device_id_type=MESH
        )
        pl.semaphore_signal(
            barrier, inc=1, device_id={"col": lax.rem(c + j, 4)}, device_id_type=MESH
        )
    for j in range(1, n_dp):
        pl.semaphore_signal(
            barrier, inc=1, device_id={"dp": lax.rem(me + j, n_dp)}, device_id_type=MESH
        )

    def pick(target, store):
        first = me * held
        count = jnp.int32(0)
        picked = [jnp.int32(0)] * per
        for i in range(requests):
            adapter = ad_ref[target, i]
            mine = (adapter >= first) & (adapter < first + held)
            for k in range(per):
                picked[k] = jnp.where(mine & (count == k), adapter - first, picked[k])
            count = count + mine.astype(jnp.int32)
        for k in range(per):
            store(k, dn_ref[picked[k]], up_ref[picked[k]])

    def keep_own(k, down, up):
        ain[me, k, 0] = down
        ain[me, k, 1] = up

    get_ad.wait()
    get_dn.wait()
    get_up.wait()
    for j in range(1, n_dp):

        def keep_out(k, down, up, j=j):
            aout[j - 1, k, 0] = down
            aout[j - 1, k, 1] = up

        pick(lax.rem(me + j, n_dp), keep_out)
    get_h.wait()

    def pass_on(b, sem, up_row):
        return remote(
            hbuf.at[b], hbuf.at[b], h_send.at[sem], h_recv.at[b], {"row": lax.rem(r + up_row, 4)}
        )

    pl.semaphore_wait(barrier, 6 + n_dp - 1)

    @pl.when(r < 3)
    def _():
        pass_on(r, 4, 1).start()

    @pl.when(r > 0)
    def _():
        pass_on(r, 5, 3).start()

    copies = []
    for j in range(1, n_dp):
        copies.append(
            remote(
                aout.at[j - 1],
                ain.at[me],
                a_send.at[j - 1],
                a_recv.at[j - 1],
                {"dp": lax.rem(me + j, n_dp)},
            )
        )
    for copy in copies:
        copy.start()
    pick(me, keep_own)
    get_len.wait()

    total = jnp.int32(0)
    for i in range(requests):
        total = total + len_ref[me, i]
    prefix = block_len - total
    starts, ends = [], []
    run = prefix
    for i in range(requests):
        starts.append(run)
        run = run + len_ref[me, i]
        ends.append(run)
    column = lax.broadcasted_iota(jnp.int32, (1, requests * rank), 1)
    col_start = jnp.zeros((1, requests * rank), jnp.int32)
    col_end = jnp.zeros((1, requests * rank), jnp.int32)
    for i in range(requests):
        here = (column >= i * rank) & (column < (i + 1) * rank)
        col_start = jnp.where(here, starts[i], col_start)
        col_end = jnp.where(here, ends[i], col_end)

    def take(b):
        @pl.when(b != r)
        def _():
            pass_on(b, b, 1).wait_recv()

        @pl.when((b < r) & (r < 3))
        def _():
            pass_on(b, b, 1).start()

        @pl.when((b > r) & (r > 0))
        def _():
            pass_on(b, b, 3).start()

    half = lax.div(r, 2)
    inner = r + half * (3 - 2 * r)
    order = []
    for step in range(4):
        b = step + inner * (1 - 2 * step) if step < 2 else step + 0 * r
        order.append(b + half * (3 - 2 * b))

    @pl.when(inner == 1)
    def _():
        take(order[1])
        take(order[2])

    for copy in copies:
        copy.wait_recv()
    holders = [lax.div(ad_ref[me, i], held) for i in range(requests)]
    for i in range(requests):
        slot = jnp.int32(0)
        for j in range(i):
            slot = slot + (holders[j] == holders[i]).astype(jnp.int32)
        pair = ain[holders[i], jnp.minimum(slot, per - 1)]
        dsel[i * rank : (i + 1) * rank, :] = pair[0]
        usel[i * rank : (i + 1) * rank, :] = pair[1]

    get_wq.wait()
    get_k.wait()
    get_v.wait()

    def part(b):
        h = hbuf[b]
        low = lax.dot_general(
            h, dsel[...], (((1,), (1,)), ((), ())), preferred_element_type=f32
        )
        pos = b * rows + lax.broadcasted_iota(jnp.int32, (rows, 1), 0)
        low = jnp.where((pos >= col_start) & (pos < col_end), low, 0.0)
        high = low.astype(bf16)
        rest = (low - high.astype(f32)).astype(bf16)
        q = jnp.dot(h, wq_ref[...], preferred_element_type=f32)
        q = q + jnp.dot(high, usel[...], preferred_element_type=f32)
        q = q + jnp.dot(rest, usel[...], preferred_element_type=f32)
        return q, jnp.dot(h, wkv_ref[...], preferred_element_type=f32)

    parts = PARTS
    span = rows // parts

    def put(slot, terms, n):
        lines = slice(n * span, (n + 1) * span)
        rs_out[slot, lines, :qcols] = terms[0].astype(bf16)
        rs_out[slot, lines, qcols:] = terms[1].astype(bf16)

    def cut(terms, n):
        lines = slice(n * span, (n + 1) * span)
        return terms[0][lines], terms[1][lines]

    def plus(terms, slot, n):
        lines = slice(n * span, (n + 1) * span)
        return (
            terms[0] + rs_in[slot, lines, :qcols].astype(f32),
            terms[1] + rs_in[slot, lines, qcols:].astype(f32),
        )

    def rs_copy(slot, device, n):
        lines = pl.ds(n * span, span)
        return remote(
            rs_out.at[slot, lines],
            rs_in.at[slot, lines],
            rs_send.at[slot, n],
            rs_recv.at[slot, n],
            {"col": device},
        )

    for step, b in enumerate(order):
        if step in (1, 2):

            @pl.when(inner == 0)
            def _():
                take(b)

        elif step == 3:
            take(b)
        odd = lax.rem(c + b, 2)
        far = lax.rem(lax.div(c, 2) + lax.div(b, 2), 2)
        terms = part(b)

        @pl.when(odd == 1)
        def _():
            for n in range(parts):
                put(1 - far, cut(terms, n), n)
                rs_copy(1 - far, sibling, n).start()

        @pl.when((odd == 0) & (far == 1))
        def _():
            for n in range(parts):
                rs_copy(0, sibling, n).wait_recv()
                put(2, plus(cut(terms, n), 0, n), n)
                rs_copy(2, across, n).start()

        @pl.when(c == b)
        def _():
            mine_sum[:, :qcols] = terms[0]
            mine_sum[:, qcols:] = terms[1]

    sums = []
    for n in range(parts):
        lines = slice(n * span, (n + 1) * span)
        rs_copy(1, sibling, n).wait_recv()
        near = plus((mine_sum[lines, :qcols], mine_sum[lines, qcols:]), 1, n)
        rs_copy(2, across, n).wait_recv()
        done = plus(near, 2, n)
        sums.append((done[0].astype(bf16), done[1].astype(bf16)))
    q = jnp.concatenate([done[0] for done in sums], axis=0)
    kv = jnp.concatenate([done[1] for done in sums], axis=0)

    keys[rows:, :] = kv
    firsts = [
        remote(
            keys.at[pl.ds(rows, PREFIX)],
            keys.at[pl.ds(0, PREFIX)],
            k_send.at[j - 1],
            k_recv.at[0],
            {"col": lax.rem(c + j, 4)},
        )
        for j in range(1, 4)
    ]
    onward = remote(
        keys.at[pl.ds(rows + PREFIX, back)],
        keys.at[pl.ds(PREFIX, back)],
        k_send.at[3],
        k_recv.at[1],
        {"col": lax.rem(c + 1, 4)},
    )
    swap = remote(
        keys.at[pl.ds(rows, rows)],
        other,
        k_send.at[4],
        k_recv.at[2],
        {"row": lax.rem(r + 2, 4)},
    )

    swap.start()

    @pl.when(c < 3)
    def _():
        onward.start()

    @pl.when(c == 0)
    def _():
        for copy in firsts:
            copy.start()
        keys[:rows, :] = jnp.zeros((rows, 2 * HEAD_DIM), bf16)

    kv_ref[:, pl.ds(k_col, HEAD_DIM)] = kv[:, :HEAD_DIM]
    kv_ref[:, pl.ds(v_col, HEAD_DIM)] = kv[:, HEAD_DIM:]

    base = c * rows
    q_pos = base + lax.broadcasted_iota(jnp.int32, (rows, 1), 0)
    seg_start = jnp.zeros((rows, 1), jnp.int32)
    for i in range(requests):
        seg_start = jnp.where(q_pos >= starts[i], starts[i], seg_start)
    at = lax.broadcasted_iota(jnp.int32, (1, 2 * rows), 1)
    k_pos = jnp.where(at < PREFIX, at, base - rows + at)
    k_pos = jnp.where((at < rows) & (c == 0), FAR, k_pos)
    allowed = (k_pos <= q_pos) & ((k_pos >= seg_start) | (k_pos < prefix))

    @pl.when(c > 0)
    def _():
        firsts[0].wait_recv()
        onward.wait_recv()

    key_rows = keys[:, :HEAD_DIM]
    value_rows = keys[:, HEAD_DIM:]
    scale = 1.0 / math.sqrt(HEAD_DIM)
    for n in range(qcols // HEAD_DIM):
        cols = slice(n * HEAD_DIM, (n + 1) * HEAD_DIM)
        score = (
            lax.dot_general(
                q[:, cols], key_rows, (((1,), (1,)), ((), ())), preferred_element_type=f32
            )
            * scale
        )
        score = jnp.where(allowed, score, -1e30)
        weight = jnp.exp(score - jnp.max(score, axis=1, keepdims=True))
        weight = jnp.where(allowed, weight, 0.0)
        row_total = jnp.sum(weight, axis=1, keepdims=True)
        mixed = jnp.dot(weight.astype(bf16), value_rows, preferred_element_type=f32)
        att_ref[:, cols] = (mixed / row_total).astype(bf16)

    swap.wait_recv()
    kv_ref[:, pl.ds(k_oth, HEAD_DIM)] = other[:, :HEAD_DIM]
    kv_ref[:, pl.ds(v_oth, HEAD_DIM)] = other[:, HEAD_DIM:]

    for copy in copies:
        copy.wait_send()
    swap.wait_send()
    for n in range(parts):
        for slot, device in ((0, sibling), (1, sibling), (2, across)):
            rs_copy(slot, device, n).wait_send()

    @pl.when(r < 3)
    def _():
        pass_on(r, 4, 1).wait_send()

    @pl.when(r > 0)
    def _():
        pass_on(r, 5, 3).wait_send()

    for b in range(4):

        @pl.when(((b < r) & (r < 3)) | ((b > r) & (r > 0)))
        def _():
            pass_on(b, b, 1).wait_send()

    @pl.when(c < 3)
    def _():
        onward.wait_send()

    @pl.when(c == 0)
    def _():
        for copy in firsts:
            copy.wait_send()


def body(hidden, w_query, w_key_value, adapter_down, adapter_up, req_lengths, req_adapter):
    n_dp = lax.axis_size("dp")
    rows, width = hidden.shape
    qcols = w_query.shape[1]
    rank = adapter_down.shape[2]
    requests = req_lengths.shape[1]
    per = (requests + n_dp - 1) // n_dp
    sums = qcols + 2 * HEAD_DIM
    bf16 = jnp.bfloat16
    vmem = pl.BlockSpec(memory_space=pltpu.VMEM)
    dma = pltpu.SemaphoreType.DMA
    return pl.pallas_call(
        functools.partial(kernel, n_dp),
        out_shape=(
            jax.ShapeDtypeStruct((rows, qcols), bf16),
            jax.ShapeDtypeStruct((rows, w_key_value.shape[1]), bf16),
        ),
        in_specs=[pl.BlockSpec(memory_space=pltpu.HBM)] * 7,
        out_specs=(vmem, vmem),
        scratch_shapes=[
            pltpu.VMEM(w_query.shape, bf16),
            pltpu.VMEM((width, 2 * HEAD_DIM), bf16),
            pltpu.VMEM((adapter_down.shape[0], rank, width), bf16),
            pltpu.VMEM(adapter_up.shape, bf16),
            pltpu.SMEM(req_lengths.shape, jnp.int32),
            pltpu.SMEM(req_adapter.shape, jnp.int32),
            dma((8,)),
            pltpu.VMEM((4, rows, width), bf16),
            pltpu.VMEM((n_dp - 1, per, 2, rank, width), bf16),
            pltpu.VMEM((n_dp, per, 2, rank, width), bf16),
            pltpu.VMEM((requests * rank, width), bf16),
            pltpu.VMEM((requests * rank, qcols), bf16),
            pltpu.VMEM((3, rows, sums), bf16),
            pltpu.VMEM((3, rows, sums), bf16),
            pltpu.VMEM((2 * rows, 2 * HEAD_DIM), bf16),
            pltpu.VMEM((rows, 2 * HEAD_DIM), bf16),
            pltpu.VMEM((rows, sums), jnp.float32),
            dma((n_dp - 1,)),
            dma((n_dp - 1,)),
            dma((6,)),
            dma((4,)),
            dma((3, PARTS)),
            dma((3, PARTS)),
            dma((5,)),
            dma((3,)),
        ],
        compiler_params=pltpu.CompilerParams(
            collective_id=0, has_side_effects=True, vmem_limit_bytes=60 << 20
        ),
    )(
        hidden,
        w_query,
        w_key_value,
        jnp.transpose(adapter_down, (0, 2, 1)),
        adapter_up,
        req_lengths,
        req_adapter,
    )


def solution(mesh):
    return jax.shard_map(
        body,
        mesh=mesh,
        in_specs=(
            P(("dp", "row"), "col"),
            P("col", "row"),
            P("col", None),
            P("dp", "col", None),
            P("dp", None, "row"),
            P(),
            P(),
        ),
        out_specs=(P(("dp", "col"), "row"), P(("dp", "col"), None)),
        check_vma=False,
    )
```
